1024 devices in a mesh: row: 8 (over z_lo), col: 16 (over x, z_hi), layer: 8 (over y, core).
Axes of the slice: x: 4, y: 4, z: 32 (z_hi: 4, z_lo: 8; z = z_hi * 8 + z_lo), core: 2. Of those that a mesh axis runs over, the one named last changes fastest.
Arguments:
- tiles: bfloat16 [8, 16, 8, 8, 1, 128, 128], P('row', 'col', 'layer'), may hold values from -2 to 2
- pair_a: int32 [8, 16, 8, 16, 16, 2], P('row', 'col', 'layer'), may hold values from 0 to 8, as said below
- pair_b: int32 [8, 16, 8, 16, 16, 2], P('row', 'col', 'layer'), may hold values from 0 to 64, as said below
Outputs:
- product: float32 [8, 16, 16, 128, 128], P('row', 'col', 'layer')
The draws below stay inside these ranges and needn't reach their ends.
Inputs may be any that keep to these rules, and one draw needn't show every extreme that they name: `pair_a`: the value 8 marks an empty product slot. For each result tile and column of the grid the live slots come first and there is at least one; in every device's list some result tile has all 2 slots live for one column and another has one. `pair_b`: equals 64 exactly where pair_a marks an empty slot.
All inputs are finite; a program needn't handle non-finite values.
Results may differ from the reference program's by a relative error of at most 0.0003.
Values may be sent and summed in bfloat16 or wider, within the bound.
No kernel may reach another device: no remote copies, remote signals or barrier semaphores. Data moves between devices by JAX's collectives and lax.ppermute only.
A program may use at most 32 MiB of HBM per device.

```python
import jax
import jax.numpy as jnp
from jax import lax

BS = 128
SB = 1
PPS = 2
S = 8
R = 16
NBP = 64
N_ROW = 8
N_COL = 16
N_LAYER = 8


def pair_live(key):
    devices_all = N_ROW * N_COL * N_LAYER
    slots = R * N_COL
    key_count, key_full, key_short = jax.random.split(key, 3)
    counts = jax.random.randint(key_count, (devices_all, slots), 1, PPS + 1)
    full_at = jax.random.randint(key_full, (devices_all, 1), 0, slots)
    short_at = (full_at + 1 + jax.random.randint(key_short, (devices_all, 1), 0, slots - 1)) % slots
    place = jnp.arange(slots, dtype=jnp.int32)[None, :]
    counts = jnp.where(place == full_at, PPS, counts)
    counts = jnp.where(place == short_at, 1, counts)
    counts = counts.reshape(N_ROW, N_COL, N_LAYER, R, N_COL, 1)
    position = jnp.arange(PPS, dtype=jnp.int32).reshape(1, 1, 1, 1, 1, PPS)
    return position < counts


def draw_pair_a(key, part):
    live = pair_live(key)
    key = jax.random.fold_in(key, 11)
    values = jax.random.randint(key, live.shape, 0, S)
    return jnp.where(live, values, S).astype(jnp.int32)


def draw_pair_b(key, part):
    live = pair_live(key)
    key = jax.random.fold_in(key, 12)
    values = jax.random.randint(key, live.shape, 0, NBP)
    return jnp.where(live, values, NBP).astype(jnp.int32)


def steps_of(stream_key, dims, cuts, smallest, high):
    loudness = 1.0
    for dim, shards_of in cuts:
        draws = jax.random.uniform(jax.random.fold_in(jax.random.fold_in(stream_key, 6), dim), (shards_of,), jnp.float32, smallest / len(cuts), high / len(cuts))
        loudness = loudness * jnp.repeat(jnp.exp(draws), dims[dim] // shards_of).reshape((-1,) + (1,) * (len(dims) - 1 - dim))
    return loudness


def bell_draw(rng, shape, deviation, bound, pieces=(), kind=jnp.bfloat16):
    result = deviation * jax.random.normal(rng, shape, jnp.float32)
    if pieces:
        result = result * steps_of(rng, shape, pieces, -0.22, 0.18)
    return jnp.clip(result, -bound, bound).astype(kind)


def setup_inputs(seed: int = 0) -> dict:
    key_list = jax.random.split(jax.random.key(seed), 4)
    return {
        "tiles": bell_draw(key_list[0], (N_ROW, N_COL, N_LAYER, N_LAYER, SB, BS, BS), 0.125, 2.0, ((0, 8), (1, 16), (2, 8))),
        "pair_a": draw_pair_a(jax.random.fold_in(key_list[3], 71), 0),
        "pair_b": draw_pair_b(jax.random.fold_in(key_list[3], 71), 0),
    }


def device_partial(tiles, pair_a, pair_b, i, j, l):
    per_dev = N_LAYER * SB
    zero_tile = jnp.zeros((1, BS, BS), jnp.float32)
    panel_a = tiles[i, :, l].reshape(N_COL * per_dev, BS, BS).astype(jnp.float32)
    panel_a = jnp.concatenate([panel_a, zero_tile], axis=0)
    panel_b = tiles[:, j, :, l].reshape(NBP, BS, BS).astype(jnp.float32)
    panel_b = jnp.concatenate([panel_b, zero_tile], axis=0)
    left = pair_a[i, j, l]
    source = jnp.arange(N_COL, dtype=jnp.int32)[None, :, None]
    index_a = jnp.where(left < per_dev, source * per_dev + left, N_COL * per_dev).astype(jnp.int32)
    index_a = index_a.reshape(R, N_COL * PPS)
    index_b = pair_b[i, j, l].reshape(R, N_COL * PPS).astype(jnp.int32)
    left_tiles = panel_a[index_a]
    right_tiles = panel_b[index_b]
    return jnp.einsum("rpik,rpkj->rij", left_tiles, right_tiles)


def reference(tiles, pair_a, pair_b):
    def grid_cell(flat):
        i = flat // N_COL
        j = flat % N_COL

        def one_layer(l):
            return device_partial(tiles, pair_a, pair_b, i, j, l)

        layered = lax.map(one_layer, jnp.arange(N_LAYER, dtype=jnp.int32))
        return jnp.sum(layered, axis=0)

    cells = lax.map(grid_cell, jnp.arange(N_ROW * N_COL, dtype=jnp.int32))
    return cells.reshape(N_ROW, N_COL, R, BS, BS)
```

```python
import functools

import jax
import jax.numpy as jnp
from jax import lax
from jax.experimental import pallas as pl
from jax.experimental.pallas import tpu as pltpu
from jax.sharding import Mesh
from jax.sharding import PartitionSpec as P

X, ZH, Y, CORE, ROW = 4, 4, 4, 2, 8
S, SLOTS, R, BS = 8, 2, 16, 128
COLS = X * ZH


def ring(n, k):
    return [(i, (i + k) % n) for i in range(n)]


def products(groups, first, place, left, right, *refs):
    parts = [len(g[2]) for g in groups]
    refs = list(refs)
    a_hbm = []
    for n in parts:
        a_hbm.append(refs[:n])
        refs = refs[n:]
    b_own, refs = refs[0], refs[1:]
    b_right, refs = refs[: ROW - 1], refs[ROW - 1 :]
    b_left, refs = refs[: ROW - 1], refs[ROW - 1 :]
    if first:
        out, a_all, b_all, a_sem, b_sem = refs
        before = None
    else:
        before, keep, send, a_all, b_all, a_sem, b_sem = refs
    x, zh, row, core, y = (place[k] for k in range(5))

    def b_copy(src, dst, s):
        return pltpu.make_async_copy(src, b_all.at[pl.ds(dst * S, S)], b_sem.at[s])

    copies = []
    n = 0
    for g, group in enumerate(groups):
        for part, (start, size) in zip(a_hbm[g], group[2]):
            copies.append(pltpu.make_async_copy(part, a_all.at[pl.ds(g * S + start, size)], a_sem.at[n]))
            n += 1
    for c in copies:
        c.start()
    b_copy(b_own, row, 0).start()
    for s in range(1, ROW):
        source = lax.rem(row - s + ROW, ROW)

        @pl.when(row >= s)
        def _(s=s, source=source):
            b_copy(b_right[s - 1], source, s).start()

        @pl.when(row < s)
        def _(s=s, source=source):
            b_copy(b_left[ROW - s - 1], source, s).start()

    zero = len(groups) * S
    a_all[zero] = jnp.zeros((BS, BS), jnp.bfloat16)
    for c in copies:
        c.wait()
    for s in range(ROW):
        b_copy(b_own, lax.rem(row - s + ROW, ROW), s).wait()

    def one(r):
        total = None if first else before[r]
        for g, (dx, dz, _) in enumerate(groups):
            c = lax.rem(x + dx, X) * ZH + lax.rem(zh + dz, ZH)
            lefts, rights = [], []
            for p in range(SLOTS):
                m = left[r, c * SLOTS + p]
                lefts.append(a_all[jnp.where(m < S, g * S + m, zero)])
                rights.append(b_all[jnp.minimum(right[r, c * SLOTS + p], ROW * S - 1)])
            value = jnp.dot(
                jnp.concatenate(lefts, axis=1),
                jnp.concatenate(rights, axis=0),
                preferred_element_type=jnp.float32,
            )
            total = value if total is None else total + value
        return total

    if first:

        @pl.loop(0, R)
        def _(r):
            out[r] = one(r)
    else:
        per = R // (Y * CORE)
        for target, other in ((send, 1), (keep, 0)):

            @pl.loop(0, Y * per)
            def _(k, target=target, other=other):
                to = lax.rem(y + k // per, Y)
                mine = lax.rem(core + other, CORE)
                target[k] = one((to * CORE + mine) * per + lax.rem(k, per))


def call(groups, place, left, right, arrays, b_arrays, before=None):
    first = before is None
    smem = pl.BlockSpec(memory_space=pltpu.SMEM)
    vmem = pl.BlockSpec(memory_space=pltpu.VMEM)
    hbm = pl.BlockSpec(memory_space=pl.ANY)
    flat = [a for group in arrays for a in group]
    operands = [place, left, right, *flat, *b_arrays]
    specs = [smem] * 3 + [hbm] * (len(flat) + len(b_arrays))
    if not first:
        operands.append(before)
        specs.append(vmem)
    half = jax.ShapeDtypeStruct((R // 2, BS, BS), jnp.float32)
    return pl.pallas_call(
        functools.partial(products, groups, first),
        out_shape=jax.ShapeDtypeStruct((R, BS, BS), jnp.float32) if first else (half, half),
        in_specs=specs,
        out_specs=vmem if first else (vmem, vmem),
        scratch_shapes=[
            pltpu.VMEM((len(groups) * S + 1, BS, BS), jnp.bfloat16),
            pltpu.VMEM((ROW * S, BS, BS), jnp.bfloat16),
            pltpu.SemaphoreType.DMA((len(flat),)),
            pltpu.SemaphoreType.DMA((ROW,)),
        ],
        compiler_params=pltpu.CompilerParams(vmem_limit_bytes=24 * 1024 * 1024),
        cost_estimate=pl.CostEstimate(
            flops=R * len(groups) * SLOTS * 2 * BS**3, bytes_accessed=4 * 1024 * 1024, transcendentals=0
        ),
    )(*operands)


def on_device(tiles, pair_a, pair_b):
    own = tiles.reshape(S, BS, BS)
    left = pair_a.reshape(R, COLS * SLOTS)
    right = pair_b.reshape(R, COLS * SLOTS)
    place = jnp.stack([lax.axis_index(n) for n in ("x", "zh", "row", "core", "y")]).astype(jnp.int32)

    def over_x(value):
        return [value] + [lax.ppermute(value, "x", ring(X, -d)) for d in range(1, X)]

    z1 = lax.ppermute(own, "zh", ring(ZH, -1))
    z3 = lax.ppermute(own, "zh", ring(ZH, 1))
    x0 = over_x(own)

    routed = lax.all_to_all(own, ("y", "core"), split_axis=0, concat_axis=0, tiled=True)
    b_right, b_left = [], []
    value = routed
    for s in range(1, ROW):
        value = lax.ppermute(value, "row", [(p, p + 1) for p in range(s - 1, ROW - 1)])
        b_right.append(value)
    value = routed
    for s in range(1, ROW):
        value = lax.ppermute(value, "row", [(p, p - 1) for p in range(1, ROW - s + 1)])
        b_left.append(value)
    b_arrays = [routed, *b_right, *b_left]

    x1 = over_x(z1)
    x3 = over_x(z3)
    half = S // 2
    z2_low = lax.ppermute(z1[:half], "zh", ring(ZH, -1))
    z2_high = lax.ppermute(z3[half:], "zh", ring(ZH, 1))
    x2_low = over_x(z2_low)
    x2_high = over_x(z2_high)

    whole = ((0, S),)
    halves = ((0, half), (half, half))
    early = [(d, z, whole) for z in (0, 1, 3) for d in range(X)]
    late = [(d, 2, halves) for d in range(X)]
    acc = call(early, place, left, right, [[a] for a in x0 + x1 + x3], b_arrays)
    keep, send = call(late, place, left, right, [[a, b] for a, b in zip(x2_low, x2_high)], b_arrays, acc)

    got = lax.ppermute(send, "core", ring(CORE, 1))
    per = R // (Y * CORE)
    quarter = [keep[d * per : (d + 1) * per] + got[d * per : (d + 1) * per] for d in range(Y)]
    total = quarter[0]
    for d in range(1, Y):
        total = total + lax.ppermute(quarter[d], "y", ring(Y, d))
    return total[None, None]


def solution(mesh):
    fine = Mesh(mesh.devices.reshape(ROW, X, ZH, Y, CORE), ("row", "x", "zh", "y", "core"))
    spec = ("row", ("x", "zh"), ("y", "core"))
    return jax.shard_map(
        on_device,
        mesh=fine,
        in_specs=(P(*spec), P(*spec), P(*spec)),
        out_specs=P(*spec),
        check_vma=False,
    )
```

```python
import functools

import jax
import jax.numpy as jnp
from jax import lax
from jax.experimental import pallas as pl
from jax.experimental.pallas import tpu as pltpu
from jax.sharding import Mesh
from jax.sharding import PartitionSpec as P

X, ZH, Y, CORE, ROW = 4, 4, 4, 2, 8
S, SLOTS, R, BS = 8, 2, 16, 128
COLS = X * ZH
PER = R // (Y * CORE)


def ring(n, k):
    return [(i, (i + k) % n) for i in range(n)]


def products(groups, unroll, place, left, right, *refs):
    n = 1 + max(g[0] for g in groups)
    a, b, refs = refs[:n], refs[n], refs[n + 1 :]
    first = len(refs) == 1
    x, zh, core, y = (place[k] for k in range(4))

    def one(r):
        total = None if first else refs[0][r]
        for array, start, dx, dz in groups:
            c = lax.rem(x + dx, X) * ZH + lax.rem(zh + dz, ZH)
            lefts, rights = [], []
            for p in range(SLOTS):
                m = left[r, c * SLOTS + p]
                tile = a[array][start + jnp.minimum(m, S - 1)]
                lefts.append(jnp.where(m < S, tile, jnp.zeros_like(tile)))
                rights.append(b[jnp.minimum(right[r, c * SLOTS + p], ROW * S - 1)])
            value = jnp.dot(
                jnp.concatenate(lefts, axis=1),
                jnp.concatenate(rights, axis=0),
                preferred_element_type=jnp.float32,
            )
            total = value if total is None else total + value
        return total

    if first:

        @pl.loop(0, R, unroll=unroll)
        def _(r):
            refs[0][r] = one(r)
    else:
        _, keep, send = refs
        for target, other in ((send, 1), (keep, 0)):

            @pl.loop(0, Y * PER, unroll=unroll)
            def _(k, target=target, other=other):
                to = lax.rem(y + k // PER, Y)
                mine = lax.rem(core + other, CORE)
                target[k] = one((to * CORE + mine) * PER + lax.rem(k, PER))


def call(groups, unroll, lists, arrays, b, *before):
    smem = pl.BlockSpec(memory_space=pltpu.SMEM)
    vmem = pl.BlockSpec(memory_space=pltpu.VMEM)
    operands = [*lists, *arrays, b, *before]
    half = jax.ShapeDtypeStruct((R // 2, BS, BS), jnp.float32)
    return pl.pallas_call(
        functools.partial(products, groups, unroll),
        out_shape=(half, half) if before else jax.ShapeDtypeStruct((R, BS, BS), jnp.float32),
        in_specs=[smem] * len(lists) + [vmem] * (len(operands) - len(lists)),
        out_specs=(vmem, vmem) if before else vmem,
        compiler_params=pltpu.CompilerParams(vmem_limit_bytes=24 * 1024 * 1024),
        cost_estimate=pl.CostEstimate(
            flops=R * len(groups) * SLOTS * 2 * BS**3, bytes_accessed=4 * 1024 * 1024, transcendentals=0
        ),
    )(*operands)


def on_device(tiles, pair_a, pair_b):
    own = tiles.reshape(S, BS, BS)
    left = pair_a.reshape(R, COLS * SLOTS)
    right = pair_b.reshape(R, COLS * SLOTS)
    place = jnp.stack([lax.axis_index(n) for n in ("x", "zh", "core", "y")]).astype(jnp.int32)
    lists = (place, left, right)

    def over_x(value):
        return [value] + [lax.ppermute(value, "x", ring(X, -d)) for d in range(1, X)]

    z1 = lax.ppermute(own, "zh", ring(ZH, -1))
    z3 = lax.ppermute(own, "zh", ring(ZH, 1))

    routed = lax.all_to_all(own, ("y", "core"), split_axis=0, concat_axis=0, tiled=True)
    b = lax.all_gather(routed, "row", axis=0, tiled=True)

    half = S // 2
    z2_low = lax.ppermute(z1[:half], "zh", ring(ZH, -1))
    z2_high = lax.ppermute(z3[half:], "zh", ring(ZH, 1))
    early = over_x(jnp.concatenate([own, z1, z3]))
    late = over_x(jnp.concatenate([z2_low, z2_high]))

    early_groups = [(d, k * S, d, z) for k, z in enumerate((0, 1, 3)) for d in range(X)]
    late_groups = [(d, 0, d, 2) for d in range(X)]
    acc = call(early_groups, 4, lists, early, b)
    keep, send = call(late_groups, 8, lists, late, b, acc)

    got = lax.ppermute(send, "core", ring(CORE, 1))
    quarter = [keep[d * PER : (d + 1) * PER] + got[d * PER : (d + 1) * PER] for d in range(Y)]
    total = quarter[0]
    for d in range(1, Y):
        total = total + lax.ppermute(quarter[d], "y", ring(Y, d))
    return total[None, None]


def solution(mesh):
    fine = Mesh(mesh.devices.reshape(ROW, X, ZH, Y, CORE), ("row", "x", "zh", "y", "core"))
    spec = ("row", ("x", "zh"), ("y", "core"))
    return jax.shard_map(
        on_device,
        mesh=fine,
        in_specs=(P(*spec), P(*spec), P(*spec)),
        out_specs=P(*spec),
        check_vma=False,
    )
```

```python
import functools

import jax
import jax.numpy as jnp
from jax import lax
from jax.experimental import pallas as pl
from jax.experimental.pallas import tpu as pltpu
from jax.sharding import Mesh
from jax.sharding import PartitionSpec as P

X, ZH, Y, CORE, ROW = 4, 4, 4, 2, 8
S, SLOTS, R, BS = 8, 2, 16, 128
COLS = X * ZH
PER = R // (Y * CORE)
QUAD = ROW // 2


def ring(n, k):
    return [(i, (i + k) % n) for i in range(n)]


def products(groups, other, place, left, right, *refs):
    n = 1 + max(g[0] for g in groups)
    a, refs = refs[:n], refs[n:]
    x, zh, core, y, row = (place[k] for k in range(5))
    if other:
        own, right_way, left_way = refs[0], refs[1:QUAD], refs[QUAD : 2 * QUAD - 1]
        out, b, sems = refs[2 * QUAD - 1 :]
        at = lax.rem(row, QUAD)

        def copy(source, s):
            slot = lax.rem(at - s + QUAD, QUAD)
            return pltpu.make_async_copy(source, b.at[pl.ds(slot * 2 * S, 2 * S)], sems.at[s])

        copy(own, 0).start()
        for s in range(1, QUAD):

            @pl.when(at >= s)
            def _(s=s):
                copy(right_way[s - 1], s).start()

            @pl.when(at < s)
            def _(s=s):
                copy(left_way[QUAD - s - 1], s).start()

        for s in range(QUAD):
            copy(own, s).wait()
    else:
        b, out = refs

    def panel_tile(t):
        t = jnp.minimum(t, ROW * S - 1)
        row_of, tile = t // S, lax.rem(t, S)
        return lax.rem(row_of, QUAD) * 2 * S + tile * 2 + row_of // QUAD

    def one(r):
        total = None
        for array, start, dx, dz in groups:
            c = lax.rem(x + dx, X) * ZH + lax.rem(zh + dz, ZH)
            lefts, rights = [], []
            for p in range(SLOTS):
                m = left[r, c * SLOTS + p]
                tile = a[array][start + jnp.minimum(m, S - 1)]
                lefts.append(jnp.where(m < S, tile, jnp.zeros_like(tile)))
                rights.append(b[panel_tile(right[r, c * SLOTS + p])])
            value = jnp.dot(
                jnp.concatenate(lefts, axis=1),
                jnp.concatenate(rights, axis=0),
                preferred_element_type=jnp.float32,
            )
            total = value if total is None else total + value
        return total

    @pl.loop(0, Y * PER, unroll=4)
    def _(k):
        to = lax.rem(y + k // PER, Y)
        mine = lax.rem(core + other, CORE)
        out[k] = one((to * CORE + mine) * PER + lax.rem(k, PER))


def call(groups, other, lists, arrays, b):
    smem = pl.BlockSpec(memory_space=pltpu.SMEM)
    vmem = pl.BlockSpec(memory_space=pltpu.VMEM)
    operands = [*lists, *arrays, *b]
    half = jax.ShapeDtypeStruct((R // 2, BS, BS), jnp.float32)
    panel = jax.ShapeDtypeStruct((ROW * S, BS, BS), jnp.bfloat16)
    return pl.pallas_call(
        functools.partial(products, groups, other),
        out_shape=(half, panel) if other else half,
        in_specs=[smem] * len(lists) + [vmem] * (len(operands) - len(lists)),
        out_specs=(vmem, vmem) if other else vmem,
        scratch_shapes=[pltpu.SemaphoreType.DMA((ROW,))] if other else [],
        compiler_params=pltpu.CompilerParams(vmem_limit_bytes=24 * 1024 * 1024),
        cost_estimate=pl.CostEstimate(
            flops=R // 2 * len(groups) * SLOTS * 2 * BS**3, bytes_accessed=8 * 1024 * 1024, transcendentals=0
        ),
    )(*operands)


def on_device(tiles, pair_a, pair_b):
    own = tiles.reshape(S, BS, BS)
    left = pair_a.reshape(R, COLS * SLOTS)
    right = pair_b.reshape(R, COLS * SLOTS)
    place = jnp.stack([lax.axis_index(n) for n in ("x", "zh", "core", "y", "row")]).astype(jnp.int32)
    lists = (place, left, right)

    def over_x(value):
        return [value] + [lax.ppermute(value, "x", ring(X, -d)) for d in range(1, X)]

    def along_z(value, k):
        at = [row * ZH + zh for zh in range(ZH) for row in range(ROW)]
        return lax.ppermute(value, ("row", "zh"), [(at[p], at[q]) for p, q in ring(ZH * ROW, k)])

    below, above = along_z(own, QUAD), along_z(own, -QUAD)
    own_x = over_x(own)
    below, above, *own_x = lax.optimization_barrier((below, above, *own_x))

    z3, z1 = along_z(below, QUAD), along_z(above, -QUAD)
    upper = lax.axis_index("row") >= QUAD
    both = jnp.stack([jnp.where(upper, below, own), jnp.where(upper, own, above)], axis=1)
    routed = lax.all_to_all(both, ("y", "core"), split_axis=0, concat_axis=0, tiled=True)
    routed = routed.reshape(2 * S, BS, BS)
    z1, z3, routed = lax.optimization_barrier((z1, z3, routed))

    half = S // 2
    z2_low = lax.ppermute(z1[:half], "zh", ring(ZH, -1))
    z2_high = lax.ppermute(z3[half:], "zh", ring(ZH, 1))

    right_way, left_way = [], []
    up = down = routed
    for s in range(1, QUAD):
        up = lax.ppermute(up, "row", [(q + p, q + p + 1) for q in (0, QUAD) for p in range(s - 1, QUAD - 1)])
        down = lax.ppermute(down, "row", [(q + p, q + p - 1) for q in (0, QUAD) for p in range(1, QUAD - s + 1)])
        if s == 1:
            up, down, z2_low, z2_high = lax.optimization_barrier((up, down, z2_low, z2_high))
        right_way.append(up)
        left_way.append(down)

    rest_x = over_x(jnp.concatenate([z1, z3, z2_low, z2_high]))
    groups = [(d, 0, d, 0) for d in range(X)]
    groups += [(X + d, k * S, d, z) for k, z in enumerate((1, 3, 2)) for d in range(X)]

    send, b = call(groups, 1, lists, own_x + rest_x, [routed, *right_way, *left_way])
    got = lax.ppermute(send, "core", ring(CORE, 1))
    keep = call(groups, 0, lists, own_x + rest_x, [b])

    quarter = [keep[d * PER : (d + 1) * PER] + got[d * PER : (d + 1) * PER] for d in range(Y)]
    total = quarter[0]
    for d in range(1, Y):
        total = total + lax.ppermute(quarter[d], "y", ring(Y, d))
    return total[None, None]


def solution(mesh):
    fine = Mesh(mesh.devices.reshape(ROW, X, ZH, Y, CORE), ("row", "x", "zh", "y", "core"))
    spec = ("row", ("x", "zh"), ("y", "core"))
    return jax.shard_map(
        on_device,
        mesh=fine,
        in_specs=(P(*spec), P(*spec), P(*spec)),
        out_specs=P(*spec),
        check_vma=False,
    )
```

```python
import functools

import jax
import jax.numpy as jnp
from jax import lax
from jax.experimental import pallas as pl
from jax.experimental.pallas import tpu as pltpu
from jax.sharding import Mesh
from jax.sharding import PartitionSpec as P

X, ZH, Y, CORE, ROW = 4, 4, 4, 2, 8
S, SLOTS, R, BS = 8, 2, 16, 128
COLS = X * ZH
WEIGHT = 7 * 10**9
PER = R // (Y * CORE)


def ring(n, k):
    return [(i, (i + k) % n) for i in range(n)]


def products(groups, other, place, left, right, *refs):
    n = 1 + max(g[0] for g in groups)
    a, refs = refs[:n], refs[n:]
    b, out = refs
    x, zh, core, y = (place[k] for k in range(4))

    def one(r):
        total = None
        for array, start, dx, dz in groups:
            c = lax.rem(x + dx, X) * ZH + lax.rem(zh + dz, ZH)
            lefts, rights = [], []
            for p in range(SLOTS):
                m = left[r, c * SLOTS + p]
                tile = a[array][start + jnp.minimum(m, S - 1)]
                lefts.append(jnp.where(m < S, tile, jnp.zeros_like(tile)))
                rights.append(b[jnp.minimum(right[r, c * SLOTS + p], ROW * S - 1)])
            value = jnp.dot(
                jnp.concatenate(lefts, axis=1),
                jnp.concatenate(rights, axis=0),
                preferred_element_type=jnp.float32,
            )
            total = value if total is None else total + value
        return total

    @pl.loop(0, Y * PER, unroll=8)
    def _(k):
        to = lax.rem(y + k // PER, Y)
        mine = lax.rem(core + other, CORE)
        out[k] = one((to * CORE + mine) * PER + lax.rem(k, PER))


def call(groups, other, lists, arrays, b):
    smem = pl.BlockSpec(memory_space=pltpu.SMEM)
    vmem = pl.BlockSpec(memory_space=pltpu.VMEM)
    operands = [*lists, *arrays, b]
    return pl.pallas_call(
        functools.partial(products, groups, other),
        out_shape=jax.ShapeDtypeStruct((R // 2, BS, BS), jnp.float32),
        in_specs=[smem] * len(lists) + [vmem] * (len(operands) - len(lists)),
        out_specs=vmem,
        compiler_params=pltpu.CompilerParams(vmem_limit_bytes=24 * 1024 * 1024),
        cost_estimate=pl.CostEstimate(
            flops=R // 2 * len(groups) * SLOTS * 2 * BS**3, bytes_accessed=8 * 1024 * 1024, transcendentals=0
        ),
    )(*operands)


def passing(place, weight, *after):
    def body(place_ref, out_ref):
        for k in range(place.shape[0]):
            out_ref[k] = place_ref[k]

    place, *after = lax.optimization_barrier((place, *after))
    smem = pl.BlockSpec(memory_space=pltpu.SMEM)
    place = pl.pallas_call(
        body,
        out_shape=jax.ShapeDtypeStruct(place.shape, place.dtype),
        in_specs=[smem],
        out_specs=smem,
        cost_estimate=pl.CostEstimate(flops=weight, bytes_accessed=1024, transcendentals=0),
    )(place)
    return place, after


def on_device(tiles, pair_a, pair_b):
    own = tiles.reshape(S, BS, BS)
    left = pair_a.reshape(R, COLS * SLOTS)
    right = pair_b.reshape(R, COLS * SLOTS)
    place = jnp.stack([lax.axis_index(n) for n in ("x", "zh", "core", "y")]).astype(jnp.int32)

    def over_x(value, after_first=False):
        got = {0: value}
        for d in (1, 3, 2):
            got[d] = lax.ppermute(value, "x", ring(X, -d))
            if after_first and d == 1:
                value, got[d] = lax.optimization_barrier((value, got[d]))
        return [got[d] for d in range(X)]

    z1 = lax.ppermute(own, "zh", ring(ZH, -1))
    z3 = lax.ppermute(own, "zh", ring(ZH, 1))
    own_x = over_x(own)
    routed = lax.all_to_all(own, ("y", "core"), split_axis=0, concat_axis=0, tiled=True)
    b = lax.all_gather(routed, "row", axis=0, tiled=True)
    z1, z3, _, *own_x = lax.optimization_barrier((z1, z3, routed, *own_x))

    half = S // 2
    z2_low = lax.ppermute(z1[:half], "zh", ring(ZH, -1))
    z2_high = lax.ppermute(z3[half:], "zh", ring(ZH, 1))
    near_x = over_x(jnp.concatenate([z1, z3]))
    far_x = over_x(jnp.concatenate([z2_low, z2_high]))
    place, arrays = passing(place, WEIGHT, *own_x, *near_x, *far_x)
    lists = (place, left, right)

    groups = [(d, 0, d, 0) for d in range(X)]
    groups += [(X + d, k * S, d, z) for k, z in enumerate((1, 3)) for d in range(X)]
    groups += [(2 * X + d, 0, d, 2) for d in range(X)]

    send = call(groups, 1, lists, arrays, b)
    keep = call(groups, 0, lists, arrays, b)
    got = lax.ppermute(send, "core", ring(CORE, 1))

    quarter = [keep[d * PER : (d + 1) * PER] + got[d * PER : (d + 1) * PER] for d in range(Y)]
    total = quarter[0]
    for d in range(1, Y):
        total = total + lax.ppermute(quarter[d], "y", ring(Y, d))
    return total[None, None]


def solution(mesh):
    fine = Mesh(mesh.devices.reshape(ROW, X, ZH, Y, CORE), ("row", "x", "zh", "y", "core"))
    spec = ("row", ("x", "zh"), ("y", "core"))
    return jax.shard_map(
        on_device,
        mesh=fine,
        in_specs=(P(*spec), P(*spec), P(*spec)),
        out_specs=P(*spec),
        check_vma=False,
    )
```

```python
import functools

import jax
import jax.numpy as jnp
from jax import lax
from jax.experimental import pallas as pl
from jax.experimental.pallas import tpu as pltpu
from jax.sharding import Mesh
from jax.sharding import PartitionSpec as P

X, ZH, Y, CORE, ROW = 4, 4, 4, 2, 8
S, SLOTS, R, BS = 8, 2, 16, 128
COLS = X * ZH
PER = R // (Y * CORE)
WEIGHT = 32 * 10**9


def ring(n, k):
    return [(i, (i + k) % n) for i in range(n)]


def products(groups, other, place, left, right, *refs):
    n = 1 + max(g[0] for g in groups)
    a, refs = refs[:n], refs[n:]
    b, out = refs
    x, zh, core, y = (place[k] for k in range(4))

    def one(r):
        total = None
        for array, start, dx, dz in groups:
            c = lax.rem(x + dx, X) * ZH + lax.rem(zh + dz, ZH)
            lefts, rights = [], []
            for p in range(SLOTS):
                m = left[r, c * SLOTS + p]
                tile = a[array][start + jnp.minimum(m, S - 1)]
                lefts.append(jnp.where(m < S, tile, jnp.zeros_like(tile)))
                rights.append(b[jnp.minimum(right[r, c * SLOTS + p], ROW * S - 1)])
            value = jnp.dot(
                jnp.concatenate(lefts, axis=1),
                jnp.concatenate(rights, axis=0),
                preferred_element_type=jnp.float32,
            )
            total = value if total is None else total + value
        return total

    @pl.loop(0, Y * PER, unroll=8)
    def _(k):
        d = k // PER
        to = y ^ d ^ (d >> 1)
        mine = lax.rem(core + other, CORE)
        out[k] = one((to * CORE + mine) * PER + lax.rem(k, PER))


def call(groups, other, lists, arrays, b):
    smem = pl.BlockSpec(memory_space=pltpu.SMEM)
    vmem = pl.BlockSpec(memory_space=pltpu.VMEM)
    return pl.pallas_call(
        functools.partial(products, groups, other),
        out_shape=jax.ShapeDtypeStruct((R // 2, BS, BS), jnp.float32),
        in_specs=[smem] * len(lists) + [vmem] * (len(arrays) + 1),
        out_specs=vmem,
        compiler_params=pltpu.CompilerParams(vmem_limit_bytes=24 * 1024 * 1024),
        cost_estimate=pl.CostEstimate(
            flops=R // 2 * len(groups) * SLOTS * 2 * BS**3, bytes_accessed=8 * 1024 * 1024, transcendentals=0
        ),
    )(*lists, *arrays, b)


def passing(place, weight, *after):
    def body(place_ref, out_ref):
        for k in range(place.shape[0]):
            out_ref[k] = place_ref[k]

    place, *after = lax.optimization_barrier((place, *after))
    smem = pl.BlockSpec(memory_space=pltpu.SMEM)
    place = pl.pallas_call(
        body,
        out_shape=jax.ShapeDtypeStruct(place.shape, place.dtype),
        in_specs=[smem],
        out_specs=smem,
        cost_estimate=pl.CostEstimate(flops=weight, bytes_accessed=1024, transcendentals=0),
    )(place)
    return place, after


def on_device(tiles, pair_a, pair_b):
    own = tiles.reshape(S, BS, BS)
    left = pair_a.reshape(R, COLS * SLOTS)
    right = pair_b.reshape(R, COLS * SLOTS)
    place = jnp.stack([lax.axis_index(n) for n in ("x", "zh", "core", "y")]).astype(jnp.int32)

    def over_x(value):
        return [value] + [lax.ppermute(value, "x", ring(X, -d)) for d in range(1, X)]

    def fenced(function, *args):
        always = lax.optimization_barrier(jnp.bool_(True))
        shapes = jax.eval_shape(function, *args)
        never = lambda *args: jax.tree.map(lambda t: jnp.zeros(t.shape, t.dtype), shapes)
        return lax.cond(always, function, never, *args)

    def together(*values):
        flat, tree = jax.tree.flatten(values)
        return jax.tree.unflatten(tree, lax.optimization_barrier(tuple(flat)))

    z1 = lax.ppermute(own, "zh", ring(ZH, -1))
    z3 = lax.ppermute(own, "zh", ring(ZH, 1))
    routed = lax.all_to_all(own, ("y", "core"), split_axis=0, concat_axis=0, tiled=True)
    b = lax.all_gather(routed, "row", axis=0, tiled=True)
    own_x = fenced(over_x, own)
    z1, z3, own_x, _ = together(z1, z3, own_x, routed)

    half = S // 2
    z2_low = lax.ppermute(z1[:half], "zh", ring(ZH, -1))
    z2_high = lax.ppermute(z3[half:], "zh", ring(ZH, 1))
    near = fenced(over_x, jnp.concatenate([z1, z3]))
    z2_low, z2_high, near = together(z2_low, z2_high, near)
    far = over_x(jnp.concatenate([z2_low, z2_high]))

    place, arrays = passing(place, WEIGHT, *own_x, *near, *far)
    lists = (place, left, right)
    groups = [(d, 0, d, 0) for d in range(X)]
    groups += [(X + d, k * S, d, z) for k, z in enumerate((1, 3)) for d in range(X)]
    groups += [(2 * X + d, 0, d, 2) for d in range(X)]
    send = call(groups, 1, lists, arrays, b)
    got = lax.ppermute(send, "core", ring(CORE, 1))
    keep = call(groups, 0, lists, arrays, b)

    half = R // 4
    mine, others = keep[:half] + got[:half], keep[half:] + got[half:]
    mine = mine + lax.ppermute(others, "y", [(k, k ^ 3) for k in range(Y)])
    total = mine[:PER] + lax.ppermute(mine[PER:], "y", [(k, k ^ 1) for k in range(Y)])
    return total[None, None]


def solution(mesh):
    fine = Mesh(mesh.devices.reshape(ROW, X, ZH, Y, CORE), ("row", "x", "zh", "y", "core"))
    spec = ("row", ("x", "zh"), ("y", "core"))
    return jax.shard_map(
        on_device,
        mesh=fine,
        in_specs=(P(*spec), P(*spec), P(*spec)),
        out_specs=P(*spec),
        check_vma=False,
    )
```

```python
import functools

import jax
import jax.numpy as jnp
from jax import lax
from jax.experimental import pallas as pl
from jax.experimental.pallas import tpu as pltpu
from jax.sharding import Mesh
from jax.sharding import PartitionSpec as P

X, ZH, Y, CORE, ROW = 4, 4, 4, 2, 8
S, SLOTS, R, BS = 8, 2, 16, 128
COLS = X * ZH
PER = R // (Y * CORE)
WEIGHT = 36 * 10**9


def ring(n, k):
    return [(i, (i + k) % n) for i in range(n)]


def products(groups, other, place, left, right, *refs):
    n = 1 + max(g[0] for g in groups)
    a, refs = refs[:n], refs[n:]
    b, out = refs
    x, zh, core, y = (place[k] for k in range(4))

    def one(r):
        total = None
        for array, start, dx, dz in groups:
            c = lax.rem(x + dx, X) * ZH + lax.rem(zh + dz, ZH)
            lefts, rights = [], []
            for p in range(SLOTS):
                m = left[r, c * SLOTS + p]
                tile = a[array][start + jnp.minimum(m, S - 1)]
                lefts.append(jnp.where(m < S, tile, jnp.zeros_like(tile)))
                rights.append(b[jnp.minimum(right[r, c * SLOTS + p], ROW * S - 1)])
            value = jnp.dot(
                jnp.concatenate(lefts, axis=1),
                jnp.concatenate(rights, axis=0),
                preferred_element_type=jnp.float32,
            )
            total = value if total is None else total + value
        return total

    @pl.loop(0, Y * PER, unroll=8)
    def _(k):
        to = lax.rem(y + k // PER, Y)
        mine = lax.rem(core + other, CORE)
        out[k] = one((to * CORE + mine) * PER + lax.rem(k, PER))


def call(groups, other, lists, arrays, b):
    smem = pl.BlockSpec(memory_space=pltpu.SMEM)
    vmem = pl.BlockSpec(memory_space=pltpu.VMEM)
    return pl.pallas_call(
        functools.partial(products, groups, other),
        out_shape=jax.ShapeDtypeStruct((R // 2, BS, BS), jnp.float32),
        in_specs=[smem] * len(lists) + [vmem] * (len(arrays) + 1),
        out_specs=vmem,
        compiler_params=pltpu.CompilerParams(vmem_limit_bytes=24 * 1024 * 1024),
        cost_estimate=pl.CostEstimate(
            flops=R // 2 * len(groups) * SLOTS * 2 * BS**3, bytes_accessed=8 * 1024 * 1024, transcendentals=0
        ),
    )(*lists, *arrays, b)


def passing(place, weight, *after):
    def body(place_ref, out_ref):
        for k in range(place.shape[0]):
            out_ref[k] = place_ref[k]

    place, *after = lax.optimization_barrier((place, *after))
    smem = pl.BlockSpec(memory_space=pltpu.SMEM)
    place = pl.pallas_call(
        body,
        out_shape=jax.ShapeDtypeStruct(place.shape, place.dtype),
        in_specs=[smem],
        out_specs=smem,
        cost_estimate=pl.CostEstimate(flops=weight, bytes_accessed=1024, transcendentals=0),
    )(place)
    return place, after


def on_device(tiles, pair_a, pair_b):
    own = tiles.reshape(S, BS, BS)
    left = pair_a.reshape(R, COLS * SLOTS)
    right = pair_b.reshape(R, COLS * SLOTS)
    place = jnp.stack([lax.axis_index(n) for n in ("x", "zh", "core", "y")]).astype(jnp.int32)

    def over_x(value):
        return [value] + [lax.ppermute(value, "x", ring(X, -d)) for d in range(1, X)]

    def fenced(function, *args):
        always = lax.optimization_barrier(jnp.bool_(True))
        shapes = jax.eval_shape(function, *args)
        never = lambda *args: jax.tree.map(lambda t: jnp.zeros(t.shape, t.dtype), shapes)
        return lax.cond(always, function, never, *args)

    def together(*values):
        flat, tree = jax.tree.flatten(values)
        return jax.tree.unflatten(tree, lax.optimization_barrier(tuple(flat)))

    z1 = lax.ppermute(own, "zh", ring(ZH, -1))
    z3 = lax.ppermute(own, "zh", ring(ZH, 1))
    routed = lax.all_to_all(own, ("y", "core"), split_axis=0, concat_axis=0, tiled=True)
    own_x = fenced(over_x, own)
    own_x, routed = together(own_x, routed)
    b = lax.all_gather(routed, "row", axis=0, tiled=True)
    z1, z3, own_x, routed = together(z1, z3, own_x, routed)

    half = S // 2
    z2_low = lax.ppermute(z1[:half], "zh", ring(ZH, -1))
    z2_high = lax.ppermute(z3[half:], "zh", ring(ZH, 1))
    near = fenced(over_x, jnp.concatenate([z1, z3]))
    place, _ = passing(place, WEIGHT, z1, z3)
    z2_low, z2_high, near, place = together(z2_low, z2_high, near, place)
    far = over_x(jnp.concatenate([z2_low, z2_high]))

    arrays = own_x + near + far
    lists = (place, left, right)
    groups = [(d, 0, d, 0) for d in range(X)]
    groups += [(X + d, k * S, d, z) for k, z in enumerate((1, 3)) for d in range(X)]
    groups += [(2 * X + d, 0, d, 2) for d in range(X)]
    send = call(groups, 1, lists, arrays, b)
    got = lax.ppermute(send, "core", ring(CORE, 1))
    keep = call(groups, 0, lists, arrays, b)

    quarter = [keep[d * PER : (d + 1) * PER] + got[d * PER : (d + 1) * PER] for d in range(Y)]
    total = quarter[0]
    for d in range(1, Y):
        total = total + lax.ppermute(quarter[d], "y", ring(Y, d))
    return total[None, None]


def solution(mesh):
    fine = Mesh(mesh.devices.reshape(ROW, X, ZH, Y, CORE), ("row", "x", "zh", "y", "core"))
    spec = ("row", ("x", "zh"), ("y", "core"))
    return jax.shard_map(
        on_device,
        mesh=fine,
        in_specs=(P(*spec), P(*spec), P(*spec)),
        out_specs=P(*spec),
        check_vma=False,
    )
```

```python
import functools

import jax
import jax.numpy as jnp
from jax import lax
from jax.experimental import pallas as pl
from jax.experimental.pallas import tpu as pltpu
from jax.sharding import Mesh
from jax.sharding import PartitionSpec as P

X, ZH, Y, CORE, ROW = 4, 4, 4, 2, 8
S, SLOTS, R, BS = 8, 2, 16, 128
COLS = X * ZH
PER = R // (Y * CORE)
STEPS = ((1, 2, 3), (4, 5, 6, 7))
ORDER = (2, 1, 3, 0)


def ring(n, k):
    return [(i, (i + k) % n) for i in range(n)]


def products(groups, far, place, left, right, *refs):
    n = 1 + max(g[0] for g in groups)
    a, refs = refs[:n], refs[n:]
    x, zh, core, y, row = (place[k] for k in range(5))
    if far == ORDER[0]:
        own, right_way, left_way = refs[0], refs[1:ROW], refs[ROW : 2 * ROW - 1]
        out, b, sems = refs[2 * ROW - 1 :]

        def copy(source, s):
            slot = lax.rem(row - s + ROW, ROW)
            return pltpu.make_async_copy(source, b.at[pl.ds(slot * S, S)], sems.at[s])

        copy(own, 0).start()
        for s in range(1, ROW):

            @pl.when(row >= s)
            def _(s=s):
                copy(right_way[s - 1], s).start()

            @pl.when(row < s)
            def _(s=s):
                copy(left_way[ROW - s - 1], s).start()

        for s in range(ROW):
            copy(own, s).wait()
    else:
        b, out = refs

    def one(r):
        total = None
        for array, start, dx, dz in groups:
            c = lax.rem(x + dx, X) * ZH + lax.rem(zh + dz, ZH)
            lefts, rights = [], []
            for p in range(SLOTS):
                m = left[r, c * SLOTS + p]
                tile = a[array][start + jnp.minimum(m, S - 1)]
                lefts.append(jnp.where(m < S, tile, jnp.zeros_like(tile)))
                rights.append(b[jnp.minimum(right[r, c * SLOTS + p], ROW * S - 1)])
            value = jnp.dot(
                jnp.concatenate(lefts, axis=1),
                jnp.concatenate(rights, axis=0),
                preferred_element_type=jnp.float32,
            )
            total = value if total is None else total + value
        return total

    to = lax.rem(y + far, Y)

    @pl.loop(0, CORE * PER, unroll=4)
    def _(k):
        on = lax.rem(core + k // PER, CORE)
        out[k] = one((to * CORE + on) * PER + lax.rem(k, PER))


def call(groups, far, lists, arrays, b):
    first = far == ORDER[0]
    smem = pl.BlockSpec(memory_space=pltpu.SMEM)
    vmem = pl.BlockSpec(memory_space=pltpu.VMEM)
    anywhere = pl.BlockSpec(memory_space=pl.ANY)
    part = jax.ShapeDtypeStruct((CORE * PER, BS, BS), jnp.float32)
    panel = jax.ShapeDtypeStruct((ROW * S, BS, BS), jnp.bfloat16)
    return pl.pallas_call(
        functools.partial(products, groups, far),
        out_shape=(part, panel) if first else part,
        in_specs=[smem] * len(lists) + [vmem] * len(arrays) + [anywhere if first else vmem] * len(b),
        out_specs=(vmem, vmem) if first else vmem,
        scratch_shapes=[pltpu.SemaphoreType.DMA((ROW,))] if first else [],
        compiler_params=pltpu.CompilerParams(vmem_limit_bytes=24 * 1024 * 1024),
        cost_estimate=pl.CostEstimate(
            flops=CORE * PER * len(groups) * SLOTS * 2 * BS**3, bytes_accessed=1024 * 1024, transcendentals=0
        ),
    )(*lists, *arrays, *b)


def on_device(tiles, pair_a, pair_b):
    own = tiles.reshape(S, BS, BS)
    left = pair_a.reshape(R, COLS * SLOTS)
    right = pair_b.reshape(R, COLS * SLOTS)
    place = jnp.stack([lax.axis_index(n) for n in ("x", "zh", "core", "y", "row")]).astype(jnp.int32)
    lists = (place, left, right)

    def over_x(value):
        return [lax.ppermute(value, "x", ring(X, -d)) for d in range(1, X)]

    def fenced(function, *args):
        always = lax.optimization_barrier(jnp.bool_(True))
        shapes = jax.eval_shape(function, *args)
        never = lambda *args: jax.tree.map(lambda t: jnp.zeros(t.shape, t.dtype), shapes)
        return lax.cond(always, function, never, *args)

    def chain(steps, up, down):
        ups, downs = [], []
        for s in steps:
            up = lax.ppermute(up, "row", [(p, p + 1) for p in range(s - 1, ROW - 1)])
            down = lax.ppermute(down, "row", [(p, p - 1) for p in range(1, ROW - s + 1)])
            ups.append(up)
            downs.append(down)
        return ups, downs

    def together(*values):
        flat, tree = jax.tree.flatten(values)
        return jax.tree.unflatten(tree, lax.optimization_barrier(tuple(flat)))

    z1 = lax.ppermute(own, "zh", ring(ZH, -1))
    z3 = lax.ppermute(own, "zh", ring(ZH, 1))
    routed = lax.all_to_all(own, ("y", "core"), split_axis=0, concat_axis=0, tiled=True)
    own_x = fenced(over_x, own)
    own_x, routed = together(own_x, routed)
    ups, downs = fenced(functools.partial(chain, STEPS[0]), routed, routed)
    z1, z3, ups, downs = together(z1, z3, ups, downs)

    half = S // 2
    z2_low = lax.ppermute(z1[:half], "zh", ring(ZH, -1))
    z2_high = lax.ppermute(z3[half:], "zh", ring(ZH, 1))
    pair = jnp.concatenate([z1, z3])
    near = fenced(over_x, pair)
    z2_low, z2_high, near, ups, downs = together(z2_low, z2_high, near, ups, downs)

    antipode = jnp.concatenate([z2_low, z2_high])
    far = over_x(antipode)
    last_ups, last_downs = fenced(functools.partial(chain, STEPS[1]), ups[-1], downs[-1])
    b = [routed, *ups, *last_ups, *downs, *last_downs]

    arrays = [own, *own_x, pair, *near, antipode, *far]
    groups = [(d, 0, d, 0) for d in range(X)]
    groups += [(X + d, k * S, d, z) for k, z in enumerate((1, 3)) for d in range(X)]
    groups += [(2 * X + d, 0, d, 2) for d in range(X)]
    parts = []
    for d in ORDER:
        if d == 0:
            place, parts[0] = together(place, parts[0])
            lists = (place, left, right)
        part = call(groups, d, lists, arrays, b)
        if d == ORDER[0]:
            part, b = part[0], [part[1]]
        parts.append(lax.ppermute(part, "y", ring(Y, d)) if d else part)
    total = sum(parts[1:], parts[0])
    return (total[:PER] + lax.ppermute(total[PER:], "core", ring(CORE, 1)))[None, None]


def solution(mesh):
    fine = Mesh(mesh.devices.reshape(ROW, X, ZH, Y, CORE), ("row", "x", "zh", "y", "core"))
    spec = ("row", ("x", "zh"), ("y", "core"))
    return jax.shard_map(
        on_device,
        mesh=fine,
        in_specs=(P(*spec), P(*spec), P(*spec)),
        out_specs=P(*spec),
        check_vma=False,
    )
```

```python
import functools

import jax
import jax.numpy as jnp
from jax import lax
from jax.experimental import pallas as pl
from jax.experimental.pallas import tpu as pltpu
from jax.sharding import Mesh
from jax.sharding import PartitionSpec as P

X, ZH, Y, CORE, ROW = 4, 4, 4, 2, 8
S, SLOTS, R, BS = 8, 2, 16, 128
COLS = X * ZH
PER = R // (Y * CORE)
WEIGHT = 36 * 10**9


def ring(n, k):
    return [(i, (i + k) % n) for i in range(n)]


def products(groups, other, place, left, right, *refs):
    n = 1 + max(array for group in groups for array, _ in group[2])
    a, refs = refs[:n], refs[n:]
    b, out = refs
    x, zh, core, y = (place[k] for k in range(4))

    def one(r):
        total = None
        for dx, dz, ((low, low_at), (high, high_at)) in groups:
            c = lax.rem(x + dx, X) * ZH + lax.rem(zh + dz, ZH)
            lefts, rights = [], []
            for p in range(SLOTS):
                m = left[r, c * SLOTS + p]
                if low == high and high_at == low_at + S // 2:
                    tile = a[low][low_at + jnp.minimum(m, S - 1)]
                else:
                    tile = jnp.where(
                        m < S // 2,
                        a[low][low_at + jnp.minimum(m, S // 2 - 1)],
                        a[high][high_at + jnp.clip(m - S // 2, 0, S // 2 - 1)],
                    )
                lefts.append(jnp.where(m < S, tile, jnp.zeros_like(tile)))
                rights.append(b[jnp.minimum(right[r, c * SLOTS + p], ROW * S - 1)])
            value = jnp.dot(
                jnp.concatenate(lefts, axis=1),
                jnp.concatenate(rights, axis=0),
                preferred_element_type=jnp.float32,
            )
            total = value if total is None else total + value
        return total

    @pl.loop(0, Y * PER, unroll=8)
    def _(k):
        to = k // PER
        mine = lax.rem(core + other, CORE)
        out[k] = one((to * CORE + mine) * PER + lax.rem(k, PER))


def call(groups, other, lists, arrays, b):
    smem = pl.BlockSpec(memory_space=pltpu.SMEM)
    vmem = pl.BlockSpec(memory_space=pltpu.VMEM)
    return pl.pallas_call(
        functools.partial(products, groups, other),
        out_shape=jax.ShapeDtypeStruct((R // 2, BS, BS), jnp.float32),
        in_specs=[smem] * len(lists) + [vmem] * (len(arrays) + 1),
        out_specs=vmem,
        compiler_params=pltpu.CompilerParams(vmem_limit_bytes=24 * 1024 * 1024),
        cost_estimate=pl.CostEstimate(
            flops=R // 2 * len(groups) * SLOTS * 2 * BS**3, bytes_accessed=8 * 1024 * 1024, transcendentals=0
        ),
    )(*lists, *arrays, b)


def passing(place, weight, *after):
    def body(place_ref, out_ref):
        for k in range(place.shape[0]):
            out_ref[k] = place_ref[k]

    place, *after = lax.optimization_barrier((place, *after))
    smem = pl.BlockSpec(memory_space=pltpu.SMEM)
    place = pl.pallas_call(
        body,
        out_shape=jax.ShapeDtypeStruct(place.shape, place.dtype),
        in_specs=[smem],
        out_specs=smem,
        cost_estimate=pl.CostEstimate(flops=weight, bytes_accessed=1024, transcendentals=0),
    )(place)
    return place, after


def on_device(tiles, pair_a, pair_b):
    own = tiles.reshape(S, BS, BS)
    left = pair_a.reshape(R, COLS * SLOTS)
    right = pair_b.reshape(R, COLS * SLOTS)
    place = jnp.stack([lax.axis_index(n) for n in ("x", "zh", "core", "y")]).astype(jnp.int32)

    def over_x(value, in_turn=False):
        got = {}
        for d in (2, 1, 3):
            got[d] = lax.ppermute(value, "x", ring(X, -d))
            if in_turn:
                value, got[d] = lax.optimization_barrier((value, got[d]))
        return [got[d] for d in range(1, X)]

    def fenced(function, *args):
        always = lax.optimization_barrier(jnp.bool_(True))
        shapes = jax.eval_shape(function, *args)
        never = lambda *args: jax.tree.map(lambda t: jnp.zeros(t.shape, t.dtype), shapes)
        return lax.cond(always, function, never, *args)

    def together(*values):
        flat, tree = jax.tree.flatten(values)
        return jax.tree.unflatten(tree, lax.optimization_barrier(tuple(flat)))

    half = S // 2
    z1_low = lax.ppermute(own[:half], "zh", ring(ZH, -1))
    z3_high = lax.ppermute(own[half:], "zh", ring(ZH, 1))
    routed = lax.all_to_all(own, ("y", "core"), split_axis=0, concat_axis=0, tiled=True)
    own_x = fenced(over_x, own)
    own_x, routed, rest = together(own_x, routed, own)
    b = lax.all_gather(routed, "row", axis=0, tiled=True)
    z1_low, z3_high, own_x, rest = together(z1_low, z3_high, own_x, rest)

    z2_low = lax.ppermute(z1_low, "zh", ring(ZH, -1))
    z2_high = lax.ppermute(z3_high, "zh", ring(ZH, 1))
    z1_high = lax.ppermute(rest[half:], "zh", ring(ZH, -1))
    z3_low = lax.ppermute(rest[:half], "zh", ring(ZH, 1))
    first = jnp.concatenate([z1_low, z3_high])
    first_x = fenced(functools.partial(over_x, in_turn=True), first)
    place, _ = passing(place, WEIGHT, z1_low, z3_high)
    z2_low, z2_high, z1_high, z3_low, first_x, place = together(z2_low, z2_high, z1_high, z3_low, first_x, place)
    last = jnp.concatenate([z2_low, z2_high, z1_high, z3_low])
    last_x = over_x(last)

    arrays = [own, *own_x, first, *first_x, last, *last_x]
    lists = (place, left, right)
    groups = []
    for d in range(X):
        at_own, at_first, at_last = d, X + d, 2 * X + d
        groups.append((d, 0, ((at_own, 0), (at_own, half))))
        groups.append((d, 1, ((at_first, 0), (at_last, 2 * half))))
        groups.append((d, 3, ((at_last, 3 * half), (at_first, half))))
        groups.append((d, 2, ((at_last, 0), (at_last, half))))
    send = call(groups, 1, lists, arrays, b)
    got = lax.ppermute(send, "core", ring(CORE, 1))
    keep = call(groups, 0, lists, arrays, b)

    parts = (keep + got).reshape(Y, PER, BS, BS)
    parts = lax.all_to_all(parts, "y", split_axis=0, concat_axis=0, tiled=True)
    return jnp.sum(parts, axis=0)[None, None]


def solution(mesh):
    fine = Mesh(mesh.devices.reshape(ROW, X, ZH, Y, CORE), ("row", "x", "zh", "y", "core"))
    spec = ("row", ("x", "zh"), ("y", "core"))
    return jax.shard_map(
        on_device,
        mesh=fine,
        in_specs=(P(*spec), P(*spec), P(*spec)),
        out_specs=P(*spec),
        check_vma=False,
    )
```

```python
import functools

import jax
import jax.numpy as jnp
from jax import lax
from jax.experimental import pallas as pl
from jax.experimental.pallas import tpu as pltpu
from jax.sharding import Mesh
from jax.sharding import PartitionSpec as P

X, ZH, Y, CORE, ROW = 4, 4, 4, 2, 8
S, SLOTS, R, BS = 8, 2, 16, 128
COLS = X * ZH
PER = R // (Y * CORE)
WEIGHT = 36 * 10**9


def ring(n, k):
    return [(i, (i + k) % n) for i in range(n)]


def products(groups, other, place, left, right, *refs):
    n = 1 + max(g[0] for g in groups)
    a, refs = refs[:n], refs[n:]
    b, out = refs
    x, zh, core, y = (place[k] for k in range(4))
    to_zh = (0, 1 + 2 * core, 3 - 2 * core, 2)

    def one(r):
        total = None
        for array, start, dx, dz in groups:
            c = lax.rem(x + dx, X) * ZH + lax.rem(zh + to_zh[dz], ZH)
            lefts, rights = [], []
            for p in range(SLOTS):
                m = left[r, c * SLOTS + p]
                tile = a[array][start + jnp.minimum(m, S - 1)]
                lefts.append(jnp.where(m < S, tile, jnp.zeros_like(tile)))
                rights.append(b[jnp.minimum(right[r, c * SLOTS + p], ROW * S - 1)])
            value = jnp.dot(
                jnp.concatenate(lefts, axis=1),
                jnp.concatenate(rights, axis=0),
                preferred_element_type=jnp.float32,
            )
            total = value if total is None else total + value
        return total

    @pl.loop(0, Y * PER, unroll=8)
    def _(k):
        to = k // PER
        mine = lax.rem(core + other, CORE)
        out[k] = one((to * CORE + mine) * PER + lax.rem(k, PER))


def call(groups, other, lists, arrays, b):
    smem = pl.BlockSpec(memory_space=pltpu.SMEM)
    vmem = pl.BlockSpec(memory_space=pltpu.VMEM)
    return pl.pallas_call(
        functools.partial(products, groups, other),
        out_shape=jax.ShapeDtypeStruct((R // 2, BS, BS), jnp.float32),
        in_specs=[smem] * len(lists) + [vmem] * (len(arrays) + 1),
        out_specs=vmem,
        compiler_params=pltpu.CompilerParams(vmem_limit_bytes=24 * 1024 * 1024),
        cost_estimate=pl.CostEstimate(
            flops=R // 2 * len(groups) * SLOTS * 2 * BS**3, bytes_accessed=8 * 1024 * 1024, transcendentals=0
        ),
    )(*lists, *arrays, b)


def passing(place, weight, *after):
    def body(place_ref, out_ref):
        for k in range(place.shape[0]):
            out_ref[k] = place_ref[k]

    place, *after = lax.optimization_barrier((place, *after))
    smem = pl.BlockSpec(memory_space=pltpu.SMEM)
    place = pl.pallas_call(
        body,
        out_shape=jax.ShapeDtypeStruct(place.shape, place.dtype),
        in_specs=[smem],
        out_specs=smem,
        cost_estimate=pl.CostEstimate(flops=weight, bytes_accessed=1024, transcendentals=0),
    )(place)
    return place, after


def on_device(tiles, pair_a, pair_b):
    own = tiles.reshape(S, BS, BS)
    left = pair_a.reshape(R, COLS * SLOTS)
    right = pair_b.reshape(R, COLS * SLOTS)
    place = jnp.stack([lax.axis_index(n) for n in ("x", "zh", "core", "y")]).astype(jnp.int32)

    def over_x(value):
        two, one, three = (lax.ppermute(value, "x", ring(X, -d)) for d in (2, 1, 3))
        return [one, two, three]

    def fenced(function, *args):
        always = lax.optimization_barrier(jnp.bool_(True))
        shapes = jax.eval_shape(function, *args)
        never = lambda *args: jax.tree.map(lambda t: jnp.zeros(t.shape, t.dtype), shapes)
        return lax.cond(always, function, never, *args)

    def together(*values):
        flat, tree = jax.tree.flatten(values)
        return jax.tree.unflatten(tree, lax.optimization_barrier(tuple(flat)))

    def along_z(value, step):
        pairs = [((z + (step if k else -step)) % ZH, z, k) for z in range(ZH) for k in range(CORE)]
        return lax.ppermute(value, ("zh", "core"), [(z * CORE + k, to * CORE + k) for to, z, k in pairs])

    n1 = along_z(own, 1)
    n2 = along_z(own, -1)
    routed = lax.all_to_all(own, ("y", "core"), split_axis=0, concat_axis=0, tiled=True)
    own_x = fenced(over_x, own)
    own_x, routed = together(own_x, routed)
    b = lax.all_gather(routed, "row", axis=0, tiled=True)
    n1, n2, own_x, routed = together(n1, n2, own_x, routed)

    opposite = along_z(n1, 1)
    both = jnp.concatenate([n1, n2])
    near = fenced(over_x, both)
    place, _ = passing(place, WEIGHT, n1, n2)
    opposite, near, place = together(opposite, near, place)
    far = over_x(opposite)

    arrays = [own, *own_x, both, *near, opposite, *far]
    lists = (place, left, right)
    groups = [(d, 0, d, 0) for d in range(X)]
    groups += [(X + d, k * S, d, z) for k, z in enumerate((1, 2)) for d in range(X)]
    groups += [(2 * X + d, 0, d, 3) for d in range(X)]
    send = call(groups, 1, lists, arrays, b)
    got = lax.ppermute(send, "core", ring(CORE, 1))
    keep = call(groups, 0, lists, arrays, b)

    parts = (keep + got).reshape(Y, PER, BS, BS)
    parts = lax.all_to_all(parts, "y", split_axis=0, concat_axis=0, tiled=True)
    return jnp.sum(parts, axis=0)[None, None]


def solution(mesh):
    fine = Mesh(mesh.devices.reshape(ROW, X, ZH, Y, CORE), ("row", "x", "zh", "y", "core"))
    spec = ("row", ("x", "zh"), ("y", "core"))
    return jax.shard_map(
        on_device,
        mesh=fine,
        in_specs=(P(*spec), P(*spec), P(*spec)),
        out_specs=P(*spec),
        check_vma=False,
    )
```

```python
import functools

import jax
import jax.numpy as jnp
from jax import lax
from jax.experimental import pallas as pl
from jax.experimental.pallas import tpu as pltpu
from jax.sharding import Mesh
from jax.sharding import PartitionSpec as P

X, ZH, Y, CORE, ROW = 4, 4, 4, 2, 8
S, SLOTS, R, BS = 8, 2, 16, 128
COLS = X * ZH
PER = R // (Y * CORE)
WEIGHT = 32 * 10**9


def ring(n, k):
    return [(i, (i + k) % n) for i in range(n)]


def products(groups, other, place, left, right, *refs):
    n = 1 + max(g[0] for g in groups)
    a, refs = refs[:n], refs[n:]
    b, out = refs
    x, zh, core, y = (place[k] for k in range(4))
    to_zh = (0, 1 + 2 * core, 3 - 2 * core, 2)

    def one(r):
        total = None
        for array, start, dx, dz in groups:
            c = lax.rem(x + dx, X) * ZH + lax.rem(zh + to_zh[dz], ZH)
            lefts, rights = [], []
            for p in range(SLOTS):
                m = left[r, c * SLOTS + p]
                tile = a[array][start + jnp.minimum(m, S - 1)]
                lefts.append(jnp.where(m < S, tile, jnp.zeros_like(tile)))
                rights.append(b[jnp.minimum(right[r, c * SLOTS + p], ROW * S - 1)])
            value = jnp.dot(
                jnp.concatenate(lefts, axis=1),
                jnp.concatenate(rights, axis=0),
                preferred_element_type=jnp.float32,
            )
            total = value if total is None else total + value
        return total

    @pl.loop(0, Y * PER, unroll=8)
    def _(k):
        to = k // PER
        mine = lax.rem(core + other, CORE)
        out[k] = one((to * CORE + mine) * PER + lax.rem(k, PER))


def call(groups, other, lists, arrays, b):
    smem = pl.BlockSpec(memory_space=pltpu.SMEM)
    vmem = pl.BlockSpec(memory_space=pltpu.VMEM)
    return pl.pallas_call(
        functools.partial(products, groups, other),
        out_shape=jax.ShapeDtypeStruct((R // 2, BS, BS), jnp.float32),
        in_specs=[smem] * len(lists) + [vmem] * (len(arrays) + 1),
        out_specs=vmem,
        compiler_params=pltpu.CompilerParams(vmem_limit_bytes=24 * 1024 * 1024),
        cost_estimate=pl.CostEstimate(
            flops=R // 2 * len(groups) * SLOTS * 2 * BS**3, bytes_accessed=8 * 1024 * 1024, transcendentals=0
        ),
    )(*lists, *arrays, b)


def passing(place, weight, *after):
    def body(place_ref, out_ref):
        for k in range(place.shape[0]):
            out_ref[k] = place_ref[k]

    place, *after = lax.optimization_barrier((place, *after))
    smem = pl.BlockSpec(memory_space=pltpu.SMEM)
    place = pl.pallas_call(
        body,
        out_shape=jax.ShapeDtypeStruct(place.shape, place.dtype),
        in_specs=[smem],
        out_specs=smem,
        cost_estimate=pl.CostEstimate(flops=weight, bytes_accessed=1024, transcendentals=0),
    )(place)
    return place, after


def on_device(tiles, pair_a, pair_b):
    own = tiles.reshape(S, BS, BS)
    left = pair_a.reshape(R, COLS * SLOTS)
    right = pair_b.reshape(R, COLS * SLOTS)
    place = jnp.stack([lax.axis_index(n) for n in ("x", "zh", "core", "y")]).astype(jnp.int32)

    def over_x(value):
        two, one, three = (lax.ppermute(value, "x", ring(X, -d)) for d in (2, 1, 3))
        return [one, two, three]

    def fenced(function, *args):
        always = lax.optimization_barrier(jnp.bool_(True))
        shapes = jax.eval_shape(function, *args)
        never = lambda *args: jax.tree.map(lambda t: jnp.zeros(t.shape, t.dtype), shapes)
        return lax.cond(always, function, never, *args)

    def together(*values):
        flat, tree = jax.tree.flatten(values)
        return jax.tree.unflatten(tree, lax.optimization_barrier(tuple(flat)))

    def along_z(value, step):
        pairs = [((z + (step if k else -step)) % ZH, z, k) for z in range(ZH) for k in range(CORE)]
        return lax.ppermute(value, ("zh", "core"), [(z * CORE + k, to * CORE + k) for to, z, k in pairs])

    n1 = along_z(own, 1)
    n2 = along_z(own, -1)
    routed = lax.all_to_all(own, ("y", "core"), split_axis=0, concat_axis=0, tiled=True)
    own_x = fenced(over_x, own)
    b = lax.all_gather(routed, "row", axis=0, tiled=True)
    n1, n2, own_x, routed = together(n1, n2, own_x, routed)

    opposite = along_z(n1, 1)
    both = jnp.concatenate([n1, n2])
    near = fenced(over_x, both)
    place, _ = passing(place, WEIGHT, n1, n2)
    opposite, near, place = together(opposite, near, place)
    far = over_x(opposite)

    arrays = [own, *own_x, both, *near, opposite, *far]
    lists = (place, left, right)
    groups = [(d, 0, d, 0) for d in range(X)]
    groups += [(X + d, k * S, d, z) for k, z in enumerate((1, 2)) for d in range(X)]
    groups += [(2 * X + d, 0, d, 3) for d in range(X)]
    send = call(groups, 1, lists, arrays, b)
    got = lax.ppermute(send, "core", ring(CORE, 1))
    keep = call(groups, 0, lists, arrays, b)

    parts = (keep + got).reshape(Y, PER, BS, BS)
    parts = lax.all_to_all(parts, "y", split_axis=0, concat_axis=0, tiled=True)
    return jnp.sum(parts, axis=0)[None, None]


def solution(mesh):
    fine = Mesh(mesh.devices.reshape(ROW, X, ZH, Y, CORE), ("row", "x", "zh", "y", "core"))
    spec = ("row", ("x", "zh"), ("y", "core"))
    return jax.shard_map(
        on_device,
        mesh=fine,
        in_specs=(P(*spec), P(*spec), P(*spec)),
        out_specs=P(*spec),
        check_vma=False,
    )
```

```python
import functools

import jax
import jax.numpy as jnp
from jax import lax
from jax.experimental import pallas as pl
from jax.experimental.pallas import tpu as pltpu
from jax.sharding import Mesh
from jax.sharding import PartitionSpec as P

X, ZH, Y, CORE, ROW = 4, 4, 4, 2, 8
S, SLOTS, R, BS = 8, 2, 16, 128
COLS = X * ZH
PER = R // (Y * CORE)
WEIGHT = 26 * 10**9


def ring(n, k):
    return [(i, (i + k) % n) for i in range(n)]


def products(groups, other, place, left, right, *refs):
    n = 1 + max(g[0] for g in groups)
    a, refs = refs[:n], refs[n:]
    b, out = refs
    x, zh, core, y = (place[k] for k in range(4))
    to_zh = (0, 1 + 2 * core, 3 - 2 * core, 2)

    def one(r):
        total = None
        for array, start, dx, dz in groups:
            c = lax.rem(x + dx, X) * ZH + lax.rem(zh + to_zh[dz], ZH)
            lefts, rights = [], []
            for p in range(SLOTS):
                m = left[r, c * SLOTS + p]
                tile = a[array][start + jnp.minimum(m, S - 1)]
                lefts.append(jnp.where(m < S, tile, jnp.zeros_like(tile)))
                rights.append(b[jnp.minimum(right[r, c * SLOTS + p], ROW * S - 1)])
            value = jnp.dot(
                jnp.concatenate(lefts, axis=1),
                jnp.concatenate(rights, axis=0),
                preferred_element_type=jnp.float32,
            )
            total = value if total is None else total + value
        return total

    @pl.loop(0, Y * PER, unroll=8)
    def _(k):
        to = k // PER
        mine = lax.rem(core + other, CORE)
        out[k] = one((to * CORE + mine) * PER + lax.rem(k, PER))


def call(groups, other, lists, arrays, b):
    smem = pl.BlockSpec(memory_space=pltpu.SMEM)
    vmem = pl.BlockSpec(memory_space=pltpu.VMEM)
    return pl.pallas_call(
        functools.partial(products, groups, other),
        out_shape=jax.ShapeDtypeStruct((R // 2, BS, BS), jnp.float32),
        in_specs=[smem] * len(lists) + [vmem] * (len(arrays) + 1),
        out_specs=vmem,
        compiler_params=pltpu.CompilerParams(vmem_limit_bytes=24 * 1024 * 1024),
        cost_estimate=pl.CostEstimate(
            flops=R // 2 * len(groups) * SLOTS * 2 * BS**3, bytes_accessed=8 * 1024 * 1024, transcendentals=0
        ),
    )(*lists, *arrays, b)


def passing(place, weight, *after):
    def body(place_ref, out_ref):
        for k in range(place.shape[0]):
            out_ref[k] = place_ref[k]

    place, *after = lax.optimization_barrier((place, *after))
    smem = pl.BlockSpec(memory_space=pltpu.SMEM)
    place = pl.pallas_call(
        body,
        out_shape=jax.ShapeDtypeStruct(place.shape, place.dtype),
        in_specs=[smem],
        out_specs=smem,
        cost_estimate=pl.CostEstimate(flops=weight, bytes_accessed=1024, transcendentals=0),
    )(place)
    return place, after


def on_device(tiles, pair_a, pair_b):
    own = tiles.reshape(S, BS, BS)
    left = pair_a.reshape(R, COLS * SLOTS)
    right = pair_b.reshape(R, COLS * SLOTS)
    place = jnp.stack([lax.axis_index(n) for n in ("x", "zh", "core", "y")]).astype(jnp.int32)

    def over_x(value):
        two, one, three = (lax.ppermute(value, "x", ring(X, -d)) for d in (2, 1, 3))
        return [one, two, three]

    def fenced(function, *args):
        always = lax.optimization_barrier(jnp.bool_(True))
        shapes = jax.eval_shape(function, *args)
        never = lambda *args: jax.tree.map(lambda t: jnp.zeros(t.shape, t.dtype), shapes)
        return lax.cond(always, function, never, *args)

    def together(*values):
        flat, tree = jax.tree.flatten(values)
        return jax.tree.unflatten(tree, lax.optimization_barrier(tuple(flat)))

    def along_z(value, step):
        pairs = [((z + (step if k else -step)) % ZH, z, k) for z in range(ZH) for k in range(CORE)]
        return lax.ppermute(value, ("zh", "core"), [(z * CORE + k, to * CORE + k) for to, z, k in pairs])

    n1 = along_z(own, 1)
    n2 = along_z(own, -1)
    routed = lax.all_to_all(own, ("y", "core"), split_axis=0, concat_axis=0, tiled=True)
    own_x = fenced(over_x, own)
    b = lax.all_gather(routed, "row", axis=0, tiled=True)
    n1, n2, own_x, routed = together(n1, n2, own_x, routed)

    opposite = along_z(n1, 1)
    both = jnp.concatenate([n1, n2])
    near = fenced(over_x, both)
    place, _ = passing(place, WEIGHT, n1, n2)
    opposite, near, place = together(opposite, near, place)
    far = over_x(opposite)

    arrays = [own, *own_x, both, *near, opposite, *far]
    lists = (place, left, right)
    groups = [(d, 0, d, 0) for d in range(X)]
    groups += [(X + d, k * S, d, z) for k, z in enumerate((1, 2)) for d in range(X)]
    groups += [(2 * X + d, 0, d, 3) for d in range(X)]
    send = call(groups, 1, lists, arrays, b)
    got = lax.ppermute(send, "core", ring(CORE, 1))
    keep = call(groups, 0, lists, arrays, b)

    parts = (keep + got).reshape(Y, PER, BS, BS)
    parts = lax.all_to_all(parts, "y", split_axis=0, concat_axis=0, tiled=True)
    return jnp.sum(parts, axis=0)[None, None]


def solution(mesh):
    fine = Mesh(mesh.devices.reshape(ROW, X, ZH, Y, CORE), ("row", "x", "zh", "y", "core"))
    spec = ("row", ("x", "zh"), ("y", "core"))
    return jax.shard_map(
        on_device,
        mesh=fine,
        in_specs=(P(*spec), P(*spec), P(*spec)),
        out_specs=P(*spec),
        check_vma=False,
    )
```

```python
import functools

import jax
import jax.numpy as jnp
from jax import lax
from jax.experimental import pallas as pl
from jax.experimental.pallas import tpu as pltpu
from jax.sharding import Mesh
from jax.sharding import PartitionSpec as P

X, ZH, Y, CORE, ROW = 4, 4, 4, 2, 8
S, SLOTS, R, BS = 8, 2, 16, 128
COLS = X * ZH
PER = R // (Y * CORE)
WEIGHT = 290 * 10**8


def ring(n, k):
    return [(i, (i + k) % n) for i in range(n)]


def products(groups, other, place, left, right, *refs):
    n = 1 + max(g[0] for g in groups)
    a, refs = refs[:n], refs[n:]
    b, out = refs
    x, zh, core, y = (place[k] for k in range(4))
    to_zh = (0, 1 + 2 * core, 3 - 2 * core, 2)

    def one(r):
        total = None
        for array, start, dx, dz in groups:
            c = lax.rem(x + dx, X) * ZH + lax.rem(zh + to_zh[dz], ZH)
            lefts, rights = [], []
            for p in range(SLOTS):
                m = left[r, c * SLOTS + p]
                tile = a[array][start + jnp.minimum(m, S - 1)]
                lefts.append(jnp.where(m < S, tile, jnp.zeros_like(tile)))
                rights.append(b[jnp.minimum(right[r, c * SLOTS + p], ROW * S - 1)])
            value = jnp.dot(
                jnp.concatenate(lefts, axis=1),
                jnp.concatenate(rights, axis=0),
                preferred_element_type=jnp.float32,
            )
            total = value if total is None else total + value
        return total

    @pl.loop(0, Y * PER, unroll=8)
    def _(k):
        to = k // PER
        mine = lax.rem(core + other, CORE)
        out[k] = one((to * CORE + mine) * PER + lax.rem(k, PER))


def call(groups, other, lists, arrays, b):
    smem = pl.BlockSpec(memory_space=pltpu.SMEM)
    vmem = pl.BlockSpec(memory_space=pltpu.VMEM)
    return pl.pallas_call(
        functools.partial(products, groups, other),
        out_shape=jax.ShapeDtypeStruct((R // 2, BS, BS), jnp.float32),
        in_specs=[smem] * len(lists) + [vmem] * (len(arrays) + 1),
        out_specs=vmem,
        compiler_params=pltpu.CompilerParams(vmem_limit_bytes=24 * 1024 * 1024),
        cost_estimate=pl.CostEstimate(
            flops=R // 2 * len(groups) * SLOTS * 2 * BS**3, bytes_accessed=8 * 1024 * 1024, transcendentals=0
        ),
    )(*lists, *arrays, b)


def passing(place, weight, *after):
    def body(place_ref, out_ref):
        for k in range(place.shape[0]):
            out_ref[k] = place_ref[k]

    place, *after = lax.optimization_barrier((place, *after))
    smem = pl.BlockSpec(memory_space=pltpu.SMEM)
    place = pl.pallas_call(
        body,
        out_shape=jax.ShapeDtypeStruct(place.shape, place.dtype),
        in_specs=[smem],
        out_specs=smem,
        cost_estimate=pl.CostEstimate(flops=weight, bytes_accessed=1024, transcendentals=0),
    )(place)
    return place, after


def on_device(tiles, pair_a, pair_b):
    own = tiles.reshape(S, BS, BS)
    left = pair_a.reshape(R, COLS * SLOTS)
    right = pair_b.reshape(R, COLS * SLOTS)
    place = jnp.stack([lax.axis_index(n) for n in ("x", "zh", "core", "y")]).astype(jnp.int32)

    def over_x(value):
        two, one, three = (lax.ppermute(value, "x", ring(X, -d)) for d in (2, 1, 3))
        return [one, two, three]

    def fenced(function, *args):
        always = lax.optimization_barrier(jnp.bool_(True))
        shapes = jax.eval_shape(function, *args)
        never = lambda *args: jax.tree.map(lambda t: jnp.zeros(t.shape, t.dtype), shapes)
        return lax.cond(always, function, never, *args)

    def together(*values):
        flat, tree = jax.tree.flatten(values)
        return jax.tree.unflatten(tree, lax.optimization_barrier(tuple(flat)))

    def along_z(value, step):
        pairs = [((z + (step if k else -step)) % ZH, z, k) for z in range(ZH) for k in range(CORE)]
        return lax.ppermute(value, ("zh", "core"), [(z * CORE + k, to * CORE + k) for to, z, k in pairs])

    n1 = along_z(own, 1)
    routed = lax.all_to_all(own, ("y", "core"), split_axis=0, concat_axis=0, tiled=True)
    b = lax.all_gather(routed, "row", axis=0, tiled=True)
    own_x = fenced(over_x, own)
    n1, own_x, again, _ = together(n1, own_x, own, routed)

    n2 = along_z(again, -1)
    opposite = along_z(n1, 1)
    first = fenced(over_x, n1)
    place, _ = passing(place, WEIGHT, n1)
    n2, opposite, first, place = together(n2, opposite, first, place)
    both = jnp.concatenate([n2, opposite])
    last = over_x(both)

    arrays = [own, *own_x, n1, *first, both, *last]
    lists = (place, left, right)
    groups = [(z * X + d, 0, d, z) for z in (0, 1) for d in range(X)]
    groups += [(2 * X + d, k * S, d, z) for k, z in enumerate((2, 3)) for d in range(X)]
    send = call(groups, 1, lists, arrays, b)
    got = lax.ppermute(send, "core", ring(CORE, 1))
    keep = call(groups, 0, lists, arrays, b)

    parts = (keep + got).reshape(Y, PER, BS, BS)
    parts = lax.all_to_all(parts, "y", split_axis=0, concat_axis=0, tiled=True)
    return jnp.sum(parts, axis=0)[None, None]


def solution(mesh):
    fine = Mesh(mesh.devices.reshape(ROW, X, ZH, Y, CORE), ("row", "x", "zh", "y", "core"))
    spec = ("row", ("x", "zh"), ("y", "core"))
    return jax.shard_map(
        on_device,
        mesh=fine,
        in_specs=(P(*spec), P(*spec), P(*spec)),
        out_specs=P(*spec),
        check_vma=False,
    )
```

```python
import functools

import jax
import jax.numpy as jnp
from jax import lax
from jax.experimental import pallas as pl
from jax.experimental.pallas import tpu as pltpu
from jax.sharding import Mesh
from jax.sharding import PartitionSpec as P

X, ZH, Y, CORE, ROW = 4, 4, 4, 2, 8
S, SLOTS, R, BS = 8, 2, 16, 128
COLS = X * ZH
PER = R // (Y * CORE)
WEIGHT = 31 * 10**9


def ring(n, k):
    return [(i, (i + k) % n) for i in range(n)]


def products(groups, other, lists, *refs):
    n = 1 + max(g[0] for g in groups)
    a, refs = refs[:n], refs[n:]
    b, out = refs
    x, zh, core, y = (lists[2 * R * COLS * SLOTS + k] for k in range(4))
    to_zh = (0, 1 + 2 * core, 3 - 2 * core, 2)

    def one(r):
        total = None
        for array, start, dx, dz in groups:
            c = lax.rem(x + dx, X) * ZH + lax.rem(zh + to_zh[dz], ZH)
            lefts, rights = [], []
            for p in range(SLOTS):
                at = (r * COLS + c) * SLOTS + p
                m = lists[at]
                tile = a[array][start + jnp.minimum(m, S - 1)]
                lefts.append(jnp.where(m < S, tile, jnp.zeros_like(tile)))
                rights.append(b[jnp.minimum(lists[R * COLS * SLOTS + at], ROW * S - 1)])
            value = jnp.dot(
                jnp.concatenate(lefts, axis=1),
                jnp.concatenate(rights, axis=0),
                preferred_element_type=jnp.float32,
            )
            total = value if total is None else total + value
        return total

    @pl.loop(0, Y * PER, unroll=8)
    def _(k):
        to = k // PER
        mine = lax.rem(core + other, CORE)
        out[k] = one((to * CORE + mine) * PER + lax.rem(k, PER))


def call(groups, other, lists, arrays, b):
    smem = pl.BlockSpec(memory_space=pltpu.SMEM)
    vmem = pl.BlockSpec(memory_space=pltpu.VMEM)
    return pl.pallas_call(
        functools.partial(products, groups, other),
        out_shape=jax.ShapeDtypeStruct((R // 2, BS, BS), jnp.float32),
        in_specs=[smem] + [vmem] * (len(arrays) + 1),
        out_specs=vmem,
        compiler_params=pltpu.CompilerParams(vmem_limit_bytes=24 * 1024 * 1024),
        cost_estimate=pl.CostEstimate(
            flops=R // 2 * len(groups) * SLOTS * 2 * BS**3, bytes_accessed=8 * 1024 * 1024, transcendentals=0
        ),
    )(lists, *arrays, b)


def passing(place, weight, *after):
    def body(place_ref, out_ref):
        for k in range(place.shape[0]):
            out_ref[k] = place_ref[k]

    place, *after = lax.optimization_barrier((place, *after))
    smem = pl.BlockSpec(memory_space=pltpu.SMEM)
    place = pl.pallas_call(
        body,
        out_shape=jax.ShapeDtypeStruct(place.shape, place.dtype),
        in_specs=[smem],
        out_specs=smem,
        cost_estimate=pl.CostEstimate(flops=weight, bytes_accessed=1024, transcendentals=0),
    )(place)
    return place, after


def on_device(tiles, pair_a, pair_b):
    own = tiles.reshape(S, BS, BS)
    pairs = jnp.concatenate([pair_a.reshape(-1), pair_b.reshape(-1)])
    place = jnp.stack([lax.axis_index(n) for n in ("x", "zh", "core", "y")]).astype(jnp.int32)

    def over_x(value):
        two, one, three = (lax.ppermute(value, "x", ring(X, -d)) for d in (2, 1, 3))
        return [one, two, three]

    def fenced(function, *args):
        always = lax.optimization_barrier(jnp.bool_(True))
        shapes = jax.eval_shape(function, *args)
        never = lambda *args: jax.tree.map(lambda t: jnp.zeros(t.shape, t.dtype), shapes)
        return lax.cond(always, function, never, *args)

    def together(*values):
        flat, tree = jax.tree.flatten(values)
        return jax.tree.unflatten(tree, lax.optimization_barrier(tuple(flat)))

    def along_z(value, step):
        pairs = [((z + (step if k else -step)) % ZH, z, k) for z in range(ZH) for k in range(CORE)]
        return lax.ppermute(value, ("zh", "core"), [(z * CORE + k, to * CORE + k) for to, z, k in pairs])

    n1 = along_z(own, 1)
    n2 = along_z(own, -1)
    routed = lax.all_to_all(own, ("y", "core"), split_axis=0, concat_axis=0, tiled=True)
    own_x = fenced(over_x, own)
    b = lax.all_gather(routed, "row", axis=0, tiled=True)
    n1, n2, own_x, routed = together(n1, n2, own_x, routed)

    opposite = along_z(n1, 1)
    both = jnp.concatenate([n1, n2])
    near = fenced(over_x, both)
    place, _ = passing(place, WEIGHT, n1, n2)
    opposite, near, place = together(opposite, near, place)
    far = over_x(opposite)

    arrays = [own, *own_x, both, *near, opposite, *far]
    lists = jnp.concatenate([pairs, place])
    groups = [(d, 0, d, 0) for d in range(X)]
    groups += [(X + d, k * S, d, z) for k, z in enumerate((1, 2)) for d in range(X)]
    groups += [(2 * X + d, 0, d, 3) for d in range(X)]
    send = call(groups, 1, lists, arrays, b)
    got = lax.ppermute(send, "core", ring(CORE, 1))
    keep = call(groups, 0, lists, arrays, b)

    parts = (keep + got).reshape(Y, PER, BS, BS)
    parts = lax.all_to_all(parts, "y", split_axis=0, concat_axis=0, tiled=True)
    return jnp.sum(parts, axis=0)[None, None]


def solution(mesh):
    fine = Mesh(mesh.devices.reshape(ROW, X, ZH, Y, CORE), ("row", "x", "zh", "y", "core"))
    spec = ("row", ("x", "zh"), ("y", "core"))
    return jax.shard_map(
        on_device,
        mesh=fine,
        in_specs=(P(*spec), P(*spec), P(*spec)),
        out_specs=P(*spec),
        check_vma=False,
    )
```

```python
import functools

import jax
import jax.numpy as jnp
from jax import lax
from jax.experimental import pallas as pl
from jax.experimental.pallas import tpu as pltpu
from jax.sharding import Mesh
from jax.sharding import PartitionSpec as P

X, ZH, Y, CORE, ROW = 4, 4, 4, 2, 8
S, SLOTS, R, BS = 8, 2, 16, 128
COLS = X * ZH
PER = R // (Y * CORE)
WEIGHT = 326 * 10**8


def ring(n, k):
    return [(i, (i + k) % n) for i in range(n)]


def products(groups, other, lists, *refs):
    n = 1 + max(g[0] for g in groups)
    a, refs = refs[:n], refs[n:]
    b, out = refs
    x, zh, core, y = (lists[2 * R * COLS * SLOTS + k] for k in range(4))
    to_zh = (0, 1 + 2 * core, 3 - 2 * core, 2)

    def one(r):
        total = None
        for array, start, dx, dz in groups:
            c = lax.rem(x + dx, X) * ZH + lax.rem(zh + to_zh[dz], ZH)
            lefts, rights = [], []
            for p in range(SLOTS):
                at = (r * COLS + c) * SLOTS + p
                m = lists[at]
                tile = a[array][start + jnp.minimum(m, S - 1)]
                lefts.append(jnp.where(m < S, tile, jnp.zeros_like(tile)))
                rights.append(b[jnp.minimum(lists[R * COLS * SLOTS + at], ROW * S - 1)])
            value = jnp.dot(
                jnp.concatenate(lefts, axis=1),
                jnp.concatenate(rights, axis=0),
                preferred_element_type=jnp.float32,
            )
            total = value if total is None else total + value
        return total

    @pl.loop(0, Y * PER, unroll=8)
    def _(k):
        to = k // PER
        mine = lax.rem(core + other, CORE)
        out[k] = one((to * CORE + mine) * PER + lax.rem(k, PER))


def call(groups, other, lists, arrays, b):
    smem = pl.BlockSpec(memory_space=pltpu.SMEM)
    vmem = pl.BlockSpec(memory_space=pltpu.VMEM)
    return pl.pallas_call(
        functools.partial(products, groups, other),
        out_shape=jax.ShapeDtypeStruct((R // 2, BS, BS), jnp.float32),
        in_specs=[smem] + [vmem] * (len(arrays) + 1),
        out_specs=vmem,
        compiler_params=pltpu.CompilerParams(vmem_limit_bytes=24 * 1024 * 1024),
        cost_estimate=pl.CostEstimate(
            flops=R // 2 * len(groups) * SLOTS * 2 * BS**3, bytes_accessed=8 * 1024 * 1024, transcendentals=0
        ),
    )(lists, *arrays, b)


def passing(place, weight, *after):
    def body(place_ref, out_ref):
        for k in range(place.shape[0]):
            out_ref[k] = place_ref[k]

    place, *after = lax.optimization_barrier((place, *after))
    smem = pl.BlockSpec(memory_space=pltpu.SMEM)
    place = pl.pallas_call(
        body,
        out_shape=jax.ShapeDtypeStruct(place.shape, place.dtype),
        in_specs=[smem],
        out_specs=smem,
        cost_estimate=pl.CostEstimate(flops=weight, bytes_accessed=1024, transcendentals=0),
    )(place)
    return place, after


def on_device(tiles, pair_a, pair_b):
    own = tiles.reshape(S, BS, BS)
    pairs = jnp.concatenate([pair_a.reshape(-1), pair_b.reshape(-1)])
    place = jnp.stack([lax.axis_index(n) for n in ("x", "zh", "core", "y")]).astype(jnp.int32)

    def over_x(value):
        two, one, three = (lax.ppermute(value, "x", ring(X, -d)) for d in (2, 1, 3))
        return [one, two, three]

    def fenced(function, *args):
        always = lax.optimization_barrier(jnp.bool_(True))
        shapes = jax.eval_shape(function, *args)
        never = lambda *args: jax.tree.map(lambda t: jnp.zeros(t.shape, t.dtype), shapes)
        return lax.cond(always, function, never, *args)

    def together(*values):
        flat, tree = jax.tree.flatten(values)
        return jax.tree.unflatten(tree, lax.optimization_barrier(tuple(flat)))

    def along_z(value, step):
        pairs = [((z + (step if k else -step)) % ZH, z, k) for z in range(ZH) for k in range(CORE)]
        return lax.ppermute(value, ("zh", "core"), [(z * CORE + k, to * CORE + k) for to, z, k in pairs])

    n1 = along_z(own, 1)
    n2 = along_z(own, -1)
    routed = lax.all_to_all(own, ("y", "core"), split_axis=0, concat_axis=0, tiled=True)
    own_x = fenced(over_x, own)
    b = lax.all_gather(routed, "row", axis=0, tiled=True)
    n1, own_x, _ = together(n1, own_x, routed)

    opposite = along_z(n1, 1)
    place, _ = passing(place, WEIGHT, n1)
    n2, place = together(n2, place)
    both = jnp.concatenate([n1, n2])
    near = fenced(over_x, both)
    opposite, near, place = together(opposite, near, place)
    far = over_x(opposite)

    arrays = [own, *own_x, both, *near, opposite, *far]
    lists = jnp.concatenate([pairs, place])
    groups = [(d, 0, d, 0) for d in range(X)]
    groups += [(X + d, k * S, d, z) for k, z in enumerate((1, 2)) for d in range(X)]
    groups += [(2 * X + d, 0, d, 3) for d in range(X)]
    send = call(groups, 1, lists, arrays, b)
    got = lax.ppermute(send, "core", ring(CORE, 1))
    keep = call(groups, 0, lists, arrays, b)

    parts = (keep + got).reshape(Y, PER, BS, BS)
    parts = lax.all_to_all(parts, "y", split_axis=0, concat_axis=0, tiled=True)
    return jnp.sum(parts, axis=0)[None, None]


def solution(mesh):
    fine = Mesh(mesh.devices.reshape(ROW, X, ZH, Y, CORE), ("row", "x", "zh", "y", "core"))
    spec = ("row", ("x", "zh"), ("y", "core"))
    return jax.shard_map(
        on_device,
        mesh=fine,
        in_specs=(P(*spec), P(*spec), P(*spec)),
        out_specs=P(*spec),
        check_vma=False,
    )
```

```python
import functools

import jax
import jax.numpy as jnp
from jax import lax
from jax.experimental import pallas as pl
from jax.experimental.pallas import tpu as pltpu
from jax.sharding import Mesh
from jax.sharding import PartitionSpec as P

X, ZH, Y, CORE, ROW = 4, 4, 4, 2, 8
S, SLOTS, R, BS = 8, 2, 16, 128
COLS = X * ZH
PER = R // (Y * CORE)
WEIGHT = 31 * 10**9


def ring(n, k):
    return [(i, (i + k) % n) for i in range(n)]


def products(groups, other, lists, *refs):
    n = 1 + max(g[0] for g in groups)
    a, refs = refs[:n], refs[n:]
    b, out = refs
    x, zh, core, y = (lists[2 * R * COLS * SLOTS + k] for k in range(4))
    to_zh = (0, 1 + 2 * core, 3 - 2 * core, 2)

    def one(r):
        total = None
        for array, start, dx, dz in groups:
            c = lax.rem(x + dx, X) * ZH + lax.rem(zh + to_zh[dz], ZH)
            lefts, rights = [], []
            for p in range(SLOTS):
                at = (r * COLS + c) * SLOTS + p
                m = lists[at]
                tile = a[array][start + jnp.minimum(m, S - 1)]
                lefts.append(jnp.where(m < S, tile, jnp.zeros_like(tile)))
                rights.append(b[jnp.minimum(lists[R * COLS * SLOTS + at], ROW * S - 1)])
            value = jnp.dot(
                jnp.concatenate(lefts, axis=1),
                jnp.concatenate(rights, axis=0),
                preferred_element_type=jnp.float32,
            )
            total = value if total is None else total + value
        return total

    @pl.loop(0, Y * PER, unroll=8)
    def _(k):
        to = k // PER
        mine = lax.rem(core + other, CORE)
        out[k] = one((to * CORE + mine) * PER + lax.rem(k, PER))


def call(groups, other, lists, arrays, b):
    smem = pl.BlockSpec(memory_space=pltpu.SMEM)
    vmem = pl.BlockSpec(memory_space=pltpu.VMEM)
    return pl.pallas_call(
        functools.partial(products, groups, other),
        out_shape=jax.ShapeDtypeStruct((R // 2, BS, BS), jnp.float32),
        in_specs=[smem] + [vmem] * (len(arrays) + 1),
        out_specs=vmem,
        compiler_params=pltpu.CompilerParams(vmem_limit_bytes=24 * 1024 * 1024),
        cost_estimate=pl.CostEstimate(
            flops=R // 2 * len(groups) * SLOTS * 2 * BS**3, bytes_accessed=8 * 1024 * 1024, transcendentals=0
        ),
    )(lists, *arrays, b)


def passing(place, weight, *after):
    def body(place_ref, out_ref):
        for k in range(place.shape[0]):
            out_ref[k] = place_ref[k]

    place, *after = lax.optimization_barrier((place, *after))
    smem = pl.BlockSpec(memory_space=pltpu.SMEM)
    place = pl.pallas_call(
        body,
        out_shape=jax.ShapeDtypeStruct(place.shape, place.dtype),
        in_specs=[smem],
        out_specs=smem,
        cost_estimate=pl.CostEstimate(flops=weight, bytes_accessed=1024, transcendentals=0),
    )(place)
    return place, after


def on_device(tiles, pair_a, pair_b):
    own = tiles.reshape(S, BS, BS)
    pairs = jnp.concatenate([pair_a.reshape(-1), pair_b.reshape(-1)])
    place = jnp.stack([lax.axis_index(n) for n in ("x", "zh", "core", "y")]).astype(jnp.int32)

    def over_x(value):
        two, one, three = (lax.ppermute(value, "x", ring(X, -d)) for d in (2, 1, 3))
        return [one, two, three]

    def fenced(function, *args):
        always = lax.optimization_barrier(jnp.bool_(True))
        shapes = jax.eval_shape(function, *args)
        never = lambda *args: jax.tree.map(lambda t: jnp.zeros(t.shape, t.dtype), shapes)
        return lax.cond(always, function, never, *args)

    def together(*values):
        flat, tree = jax.tree.flatten(values)
        return jax.tree.unflatten(tree, lax.optimization_barrier(tuple(flat)))

    def along_z(value, step):
        pairs = [((z + (step if k else -step)) % ZH, z, k) for z in range(ZH) for k in range(CORE)]
        return lax.ppermute(value, ("zh", "core"), [(z * CORE + k, to * CORE + k) for to, z, k in pairs])

    n1 = along_z(own, 1)
    n2 = along_z(own, -1)
    routed = lax.all_to_all(own, ("y", "core"), split_axis=0, concat_axis=0, tiled=True)
    own_x = fenced(over_x, own)
    b = lax.all_gather(routed, "row", axis=0, tiled=True)
    n1, own_x, _ = together(n1, own_x, routed)

    opposite = along_z(n1, 1)
    place, _ = passing(place, WEIGHT, n1)
    n2, place = together(n2, place)
    both = jnp.concatenate([n1, n2])
    near = fenced(over_x, both)
    opposite, near, place = together(opposite, near, place)
    far = over_x(opposite)

    arrays = [own, *own_x, both, *near, opposite, *far]
    lists = jnp.concatenate([pairs, place])
    groups = [(d, 0, d, 0) for d in range(X)]
    groups += [(X + d, k * S, d, z) for k, z in enumerate((1, 2)) for d in range(X)]
    groups += [(2 * X + d, 0, d, 3) for d in range(X)]
    send = call(groups, 1, lists, arrays, b)
    got = lax.ppermute(send, "core", ring(CORE, 1))
    keep = call(groups, 0, lists, arrays, b)

    parts = (keep + got).reshape(Y, PER, BS, BS)
    parts = lax.all_to_all(parts, "y", split_axis=0, concat_axis=0, tiled=True)
    return jnp.sum(parts, axis=0)[None, None]


def solution(mesh):
    fine = Mesh(mesh.devices.reshape(ROW, X, ZH, Y, CORE), ("row", "x", "zh", "y", "core"))
    spec = ("row", ("x", "zh"), ("y", "core"))
    return jax.shard_map(
        on_device,
        mesh=fine,
        in_specs=(P(*spec), P(*spec), P(*spec)),
        out_specs=P(*spec),
        check_vma=False,
    )
```
